256 devices in a mesh: dp: 8 (over x, core), expert: 32 (over y, z).
Axes of the slice: x: 4, y: 4, z: 8, core: 2. Of those that a mesh axis runs over, the one named last changes fastest.
Arguments:
- dense_weights: bfloat16 [3, 5632, 2048], P(None, 'dp', 'expert'), may hold values from -0.125 to 0.125
- tokens: bfloat16 [4096, 2048], P('expert'), may hold values from -6 to 6
- cotangent: bfloat16 [4096, 2048], P('expert'), may hold values from -6 to 6
- routes: int32 [4096, 4], P('expert'), may hold values from 0 to 31, all different within a row; in each aligned block of 128 rows (0 to 127, 128 to 255, ...) at most 20 rows name the same one
- route_gates: float32 [4096, 4], P('expert'), may hold values from 0.2 to 1
- unit_perm: int32 [8, 5632], replicated, may hold values from 0 to 5631, as said below
- slab_owner: int32 [32], replicated, may hold values from 0 to 31, each once
Outputs:
- mixed: bfloat16 [4096, 2048], P('expert', 'dp')
- token_grad: bfloat16 [4096, 2048], P('expert', 'dp')
- expert_grad: bfloat16 [32, 3, 1408, 2048], P('expert', None, 'dp')
The draws below stay inside these ranges and needn't reach their ends.
Inputs may be any that keep to these rules, and one draw needn't show every extreme that they name: `unit_perm`: each row is a permutation of the 5632 units. In every row, for every slab s and share g, the 176 positions s * 1408 + g * 176 up to s * 1408 + (g + 1) * 176 - 1 hold exactly 22 units of each block of 704 consecutive units. `slab_owner`: each slab number c * 4 + s is owned by exactly one expert. `routes`: each row names 4 different experts. In each aligned block of 128 rows no expert is named more than 20 times, a bound that some block reaches.
All inputs are finite; a program needn't handle non-finite values.
Results may differ from the reference program's by a relative error of at most 0.013.
Values may be sent and summed in bfloat16 or wider, within the bound.
No kernel may reach another device: no remote copies, remote signals or barrier semaphores. Data moves between devices by JAX's collectives and lax.ppermute only.
A program may use at most 128 MiB of HBM per device.

```python
import math
import jax
import jax.numpy as jnp
import numpy as np
from jax import lax

D = 2048
FF = 5632
EH = 1408
TOPK = 4
TOK_DEV = 128
EXPERTS = 32
SLABS = 4
COPIES = 8
UNITS_DEV = 176
PICK = 22
CAP = 20
TOKENS = 4096
N_DP = 8
N_EXPERT = 32


def draw_unit_perm(key, part):
    block_units = FF // N_DP
    key_list = jax.random.split(key, COPIES * N_DP)
    local_order = jax.vmap(lambda subkey: jax.random.permutation(subkey, block_units))(key_list)
    local_order = local_order.reshape(COPIES, N_DP, SLABS * N_DP, PICK).astype(jnp.int32)
    offsets = (jnp.arange(N_DP, dtype=jnp.int32) * block_units)[None, :, None, None]
    unit_ids = local_order + offsets
    unit_ids = jnp.transpose(unit_ids, (0, 2, 1, 3)).reshape(COPIES, SLABS * N_DP, UNITS_DEV)
    second_keys = jax.random.split(jax.random.fold_in(key, 7), COPIES * SLABS * N_DP)
    pair_order = jax.vmap(lambda subkey: jax.random.permutation(subkey, UNITS_DEV))(second_keys)
    pair_order = pair_order.reshape(COPIES, SLABS * N_DP, UNITS_DEV).astype(jnp.int32)
    unit_ids = jnp.take_along_axis(unit_ids, pair_order, axis=2)
    return unit_ids.reshape(COPIES, FF).astype(jnp.int32)


def block_scale(stream_key, shape, cuts, least, largest):
    def one(axis_at, parts):
        draws = jax.random.uniform(jax.random.fold_in(jax.random.fold_in(stream_key, 6), axis_at), (parts,), jnp.float32, least / len(cuts), largest / len(cuts))
        return jnp.repeat(jnp.exp(draws), shape[axis_at] // parts).reshape((-1,) + (1,) * (len(shape) - axis_at - 1))

    level = one(*cuts[0])
    for cut in cuts[1:]:
        level = level * one(*cut)
    return level


def assign_block(rng, own, number, rows, amount, top, bound, slope):
    order = jax.random.permutation(rng, amount)
    crowded, usual = shares(amount, rows * top, bound, slope, True), shares(amount, rows * top, bound, slope, False)
    places = jnp.arange(amount)

    def named(lengths, offset_by):
        used = int((lengths > 0).sum())
        fixed = max(1, used // 4)
        shifted = fixed + (places - fixed + offset_by * (used - fixed)) % max(1, amount - fixed)
        return jnp.zeros((amount,), jnp.int32).at[order[jnp.where(places < fixed, places, shifted)]].set(jnp.asarray(lengths, jnp.int32))

    lengths = jnp.where(number % 4 == 0, named(crowded, number // 4), named(usual, number - number // 4 - 1))
    mixed = jax.random.permutation(jax.random.fold_in(own, 3), amount)
    giver, sink = mixed[0:amount // 2 * 2:2], mixed[1:amount // 2 * 2:2]
    slack = jnp.minimum(lengths[giver] - 1, bound - lengths[sink]) // 2
    slack = jnp.where((giver == order[0]) | (sink == order[0]) | (lengths[sink] == 0), 0, jnp.maximum(slack, 0))
    shifted = jax.random.randint(jax.random.fold_in(own, 4), (amount // 2,), 0, 1 << 20) % (slack + 1)
    lengths = lengths.at[giver].add(-shifted).at[sink].add(shifted)
    labels = jnp.searchsorted(jnp.cumsum(lengths), jnp.arange(rows * top), side="right").astype(jnp.int32)
    table = labels.reshape(top, rows).T
    table = table[jax.random.permutation(jax.random.fold_in(own, 1), rows)]
    offset_by = jax.random.randint(jax.random.fold_in(own, 2), (rows, 1), 0, top)
    return jnp.take_along_axis(table, (jnp.arange(top)[None, :] + offset_by) % top, axis=1)


def shares(number_of, total, bound, slope, full):
    loads = [(1 << 20) // math.isqrt(grade ** slope) + 1 for grade in range(1, number_of + 1)]
    largest = bound if full else min(bound, max(-(-total // number_of), total * loads[0] // sum(loads)))
    least = 1 if total - largest >= number_of - 1 else 0
    given, spare = [largest] + [least] * (number_of - 1), total - largest - least * (number_of - 1)
    while spare > 0:
        movable = [i for i in range(1, number_of) if given[i] < largest] or [i for i in range(1, number_of) if given[i] < bound]
        pool, left = sum([loads[i] for i in movable]), spare
        for i in movable:
            addition = min(bound - given[i], max(1, left * loads[i] // pool), spare)
            given[i] = given[i] + addition
            spare = spare - addition
    return np.array(given)


def gaussian(rng, extent, scale, most, pieces=(), kind=jnp.bfloat16):
    loudness = block_scale(rng, extent, pieces, -0.22, 0.18) if pieces else 1.0
    values = jax.random.normal(rng, extent, jnp.float32) * scale * loudness
    return jnp.minimum(jnp.maximum(values, -most), most).astype(kind)


def setup_inputs(seed: int = 0) -> dict:
    streams_of = jax.random.split(jax.random.key(seed), 8)
    dense_weights = gaussian(streams_of[0], (3, FF, D), D ** -0.5, 0.125, ((1, 8), (2, 32)))
    tokens = gaussian(streams_of[1], (TOKENS, D), 1.0, 6.0, ((0, 32),))
    cotangent = gaussian(streams_of[2], (TOKENS, D), 1.0, 6.0, ((0, 32),))
    routes_keys = jax.random.split(jax.random.fold_in(streams_of[3], 1), TOKENS // TOK_DEV)
    routes_turns = jax.random.permutation(jax.random.fold_in(streams_of[3], 3), TOKENS // TOK_DEV)
    routes = jax.vmap(lambda own, number: assign_block(jax.random.fold_in(streams_of[3], 2), own, number, TOK_DEV, EXPERTS, TOPK, CAP, 1))(routes_keys, routes_turns).reshape((TOKENS, TOPK))
    route_gates = jnp.clip(0.2 + 0.8 * jax.random.uniform(streams_of[4], (TOKENS, TOPK), jnp.float32) ** block_scale(streams_of[4], (TOKENS, TOPK), ((0, 32),), -0.2, 0.2), 0.2, 1.0)
    unit_perm = draw_unit_perm(jax.random.fold_in(streams_of[7], 71), 0)
    slab_owner = jax.random.permutation(streams_of[6], EXPERTS).astype(jnp.int32)
    return dict(dense_weights=dense_weights, tokens=tokens, cotangent=cotangent, routes=routes, route_gates=route_gates, unit_perm=unit_perm, slab_owner=slab_owner)


def silu_parts(preact):
    sigmoid_value = jax.nn.sigmoid(preact)
    return preact * sigmoid_value, sigmoid_value * (1.0 + preact * (1.0 - sigmoid_value))


def share_products(left_side, weights):
    left_f = left_side.astype(jnp.float32).reshape(left_side.shape[0], N_DP, UNITS_DEV)
    right_f = weights.astype(jnp.float32).reshape(N_DP, UNITS_DEV, D)
    return jnp.einsum("sgu,gud->sgd", left_f, right_f)


def round_sum(share_parts):
    rounded = lax.optimization_barrier(share_parts.astype(jnp.bfloat16))
    return jnp.sum(rounded.astype(jnp.float32), axis=1)


def reference(dense_weights, tokens, cotangent, routes, route_gates, unit_perm, slab_owner):
    shared_gate = jnp.dot(tokens, dense_weights[0].T, preferred_element_type=jnp.float32)
    shared_up = jnp.dot(tokens, dense_weights[1].T, preferred_element_type=jnp.float32)
    shared_act, shared_slope = silu_parts(shared_gate)
    shared_hidden = (shared_act * shared_up).astype(jnp.bfloat16)
    shared_out = jnp.dot(shared_hidden, dense_weights[2], preferred_element_type=jnp.float32)
    shared_dh = jnp.dot(cotangent, dense_weights[2].T, preferred_element_type=jnp.float32)
    shared_dgate = (shared_dh * shared_up * shared_slope).astype(jnp.bfloat16)
    shared_dup = (shared_dh * shared_act).astype(jnp.bfloat16)
    shared_back = jnp.dot(shared_dgate, dense_weights[0], preferred_element_type=jnp.float32) + jnp.dot(shared_dup, dense_weights[1], preferred_element_type=jnp.float32)

    copies = TOKENS * TOPK
    flat_routes = routes.reshape(-1).astype(jnp.int32)
    onehot = (flat_routes[:, None] == jnp.arange(EXPERTS, dtype=jnp.int32)[None, :]).astype(jnp.int32)
    running = jnp.cumsum(onehot.reshape(N_EXPERT, TOK_DEV * TOPK, EXPERTS), axis=1).reshape(copies, EXPERTS)
    slot_rank = jnp.sum((running - 1) * onehot, axis=1)
    block_of = jnp.arange(copies, dtype=jnp.int32) // (TOK_DEV * TOPK)
    slot_index = (block_of * CAP + slot_rank).astype(jnp.int32)
    slot_table = jnp.full((EXPERTS, N_EXPERT * CAP), copies, jnp.int32).at[flat_routes, slot_index].set(jnp.arange(copies, dtype=jnp.int32))
    flat_gates = route_gates.reshape(-1)

    def expert_step(packed):
        expert, slot_rows = packed
        owned_slab = slab_owner[expert]
        copy_id = (owned_slab // SLABS).astype(jnp.int32)
        slab_start = ((owned_slab % SLABS) * EH).astype(jnp.int32)
        unit_ids = lax.dynamic_slice(unit_perm, (copy_id, slab_start), (1, EH))[0]
        weights = jnp.take(dense_weights, unit_ids, axis=1)
        filled = slot_rows < copies
        safe_rows = jnp.minimum(slot_rows, copies - 1)
        token_of = safe_rows // TOPK
        copy_x = jnp.where(filled[:, None], tokens[token_of], jnp.zeros((), jnp.bfloat16))
        gate_of = jnp.where(filled, flat_gates[safe_rows], jnp.zeros((), jnp.float32))
        copy_dy = (gate_of[:, None] * cotangent[token_of].astype(jnp.float32)).astype(jnp.bfloat16)
        pre_gate = jnp.dot(copy_x, weights[0].T, preferred_element_type=jnp.float32)
        pre_up = jnp.dot(copy_x, weights[1].T, preferred_element_type=jnp.float32)
        activation, silu_slope = silu_parts(pre_gate)
        hidden = (activation * pre_up).astype(jnp.bfloat16)
        out_rows = round_sum(share_products(hidden, weights[2]))
        d_hidden = jnp.dot(copy_dy, weights[2].T, preferred_element_type=jnp.float32)
        d_gate = (d_hidden * pre_up * silu_slope).astype(jnp.bfloat16)
        d_up = (d_hidden * activation).astype(jnp.bfloat16)
        back_rows = round_sum(share_products(d_gate, weights[0]) + share_products(d_up, weights[1]))
        weight_grads = jnp.stack([
            jnp.dot(d_gate.T, copy_x, preferred_element_type=jnp.float32),
            jnp.dot(d_up.T, copy_x, preferred_element_type=jnp.float32),
            jnp.dot(hidden.T, copy_dy, preferred_element_type=jnp.float32),
        ]).astype(jnp.bfloat16)
        return out_rows, back_rows, weight_grads

    out_rows, back_rows, expert_grad = lax.map(expert_step, (jnp.arange(EXPERTS, dtype=jnp.int32), slot_table))
    routed_out = out_rows[flat_routes, slot_index].reshape(TOKENS, TOPK, D)
    routed_back = back_rows[flat_routes, slot_index].reshape(TOKENS, TOPK, D)
    mixed = (shared_out + jnp.sum(route_gates[:, :, None] * routed_out, axis=1)).astype(jnp.bfloat16)
    token_grad = (shared_back + jnp.sum(routed_back, axis=1)).astype(jnp.bfloat16)
    return mixed, token_grad, expert_grad
```

```python
import jax
import jax.numpy as jnp
import numpy as np
from jax import lax
from jax.experimental import pallas as pl
from jax.experimental.pallas import tpu as pltpu
from jax.sharding import Mesh, PartitionSpec as P

NX, NC, NY, NZ = 4, 2, 4, 8
DP, EXPERT = ("x", "c"), ("y", "z")
SIZE = {"x": NX, "c": NC, "y": NY, "z": NZ}
D = 2048
EH = 1408
UNITS = 704
HALF = UNITS // 2
SHARE = 176
PICK = 22
PAD = 32
CAP = 20
TOK = 128
N_DP, N_EXP = 8, 32
SLOTS = N_EXP * CAP
ROWS = 2 * SLOTS
COLS = D // N_DP
PART_A = 640
PART_B = 3 * HALF - PART_A
F32, BF16 = jnp.float32, jnp.bfloat16
VMEM_LIMIT = 60 * 1024 * 1024
Z_FROM = (0, -1, 1, -2, 2, -3, 3, 4)
Y_FROM = (0, -1, 1, 2)


def shift(value, axis, by):
    size = SIZE[axis]
    return lax.ppermute(value, axis, [(i, (i + by) % size) for i in range(size)])


def dot(lhs, rhs):
    return jnp.dot(lhs, rhs, preferred_element_type=F32)


def dot_last(lhs, rhs):
    return lax.dot_general(lhs, rhs, (((1,), (1,)), ((), ())), preferred_element_type=F32)


def dot_first(lhs, rhs):
    return lax.dot_general(lhs, rhs, (((0,), (0,)), ((), ())), preferred_element_type=F32)


def split3(value):
    high = value.astype(BF16)
    rest = value - high.astype(F32)
    middle = rest.astype(BF16)
    return high, middle, (rest - middle.astype(F32)).astype(BF16)


def silu_parts(preact):
    sigmoid_value = jax.nn.sigmoid(preact)
    return preact * sigmoid_value, sigmoid_value * (1.0 + preact * (1.0 - sigmoid_value))


def vmem():
    return pl.BlockSpec(memory_space=pltpu.VMEM)


def smem():
    return pl.BlockSpec(memory_space=pltpu.SMEM)


def hbm():
    return pl.BlockSpec(memory_space=pl.ANY)


def params():
    return pltpu.CompilerParams(vmem_limit_bytes=VMEM_LIMIT)


def slot_columns():
    column = np.arange(ROWS)
    table = np.zeros((8, ROWS), np.int32)
    table[0] = column // (2 * CAP)
    table[1] = column % (2 * CAP) // CAP
    table[2] = column % CAP
    return jnp.asarray(table)


def order_matrix():
    matrix = np.zeros((160, 160), np.float32)
    for b in range(4):
        for p in range(2):
            for r in range(CAP):
                matrix[p * 80 + b * CAP + r, b * 40 + p * CAP + r] = 1
    return jnp.asarray(matrix, BF16)


def pair_matrix():
    matrix = np.zeros((256, 256), np.float32)
    for i in range(64):
        matrix[i, i] = 1
        matrix[64 + i, 128 + i] = 1
        matrix[128 + i, 64 + i] = 1
        matrix[192 + i, 192 + i] = 1
    return jnp.asarray(matrix, BF16)


def slot_masks(routes_ref, gates_ref, table_ref):
    expert = table_ref[0:1, :]
    part = table_ref[1:2, :]
    rank = table_ref[2:3, :].astype(F32)
    named = jnp.zeros((TOK, ROWS), F32)
    gate = jnp.zeros((TOK, ROWS), F32)
    for k in range(4):
        hit = routes_ref[:, k : k + 1] == expert
        named = named + jnp.where(hit, 1.0, 0.0)
        gate = gate + jnp.where(hit, gates_ref[:, k : k + 1], 0.0)
    row = lax.broadcasted_iota(jnp.int32, (TOK, TOK), 0)
    col = lax.broadcasted_iota(jnp.int32, (TOK, TOK), 1)
    before = jnp.where(col < row, 1.0, 0.0).astype(BF16)
    place = dot(before, named.astype(BF16))
    slot = jnp.where((place == rank) & (named > 0.5), 1.0, 0.0)
    first = jnp.where(part == 0, slot, 0.0)
    second = jnp.where(part == 1, slot, 0.0)
    return first, second, gate


def send_kernel(place_ref, routes_ref, gates_ref, table_ref, tokens_ref, cot_ref, out_ref):
    first, second, gate = slot_masks(routes_ref, gates_ref, table_ref)
    columns = pl.ds(pl.multiple_of(place_ref[0] * COLS, COLS), COLS)
    rows_x = dot_first(first.astype(BF16), tokens_ref[:, columns])
    rows_dy = dot_first(second.astype(BF16), cot_ref[:, columns])
    ones = jnp.ones((TOK, COLS), BF16)
    scale = jnp.zeros((ROWS, COLS), F32)
    for piece in split3(second * gate):
        scale = scale + dot_first(piece, ones)
    out_ref[...] = (rows_x + rows_dy * scale).astype(BF16)


def order_in_kernel(order_ref, in_ref, out_ref):
    for b in range(8):
        rows = dot(order_ref[...], in_ref[160 * b : 160 * (b + 1), :]).astype(BF16)
        out_ref[80 * b : 80 * (b + 1), :] = rows[:80]
        out_ref[SLOTS + 80 * b : SLOTS + 80 * (b + 1), :] = rows[80:]


def order_out_kernel(order_ref, in_ref, out_ref):
    for b in range(8):
        rows = jnp.concatenate(
            [in_ref[80 * b : 80 * (b + 1), :], in_ref[SLOTS + 80 * b : SLOTS + 80 * (b + 1), :]],
            axis=0,
        )
        out_ref[160 * b : 160 * (b + 1), :] = dot_first(order_ref[...], rows).astype(BF16)


def combine_kernel(routes_ref, gates_ref, table_ref, back_ref, sums_ref, mixed_ref, grad_ref):
    first, second, gate = slot_masks(routes_ref, gates_ref, table_ref)
    rows = back_ref[...]
    mixed = sums_ref[ROWS : ROWS + TOK, :].astype(F32)
    for piece in split3(first * gate):
        mixed = mixed + dot(piece, rows)
    mixed_ref[...] = mixed.astype(BF16)
    grad = sums_ref[ROWS + TOK : ROWS + 2 * TOK, :].astype(F32) + dot(second.astype(BF16), rows)
    grad_ref[...] = grad.astype(BF16)


def block_copies(refs, gathered, place_ref, sems):
    a_refs, b_refs = refs[:5], refs[5:]
    y, z = place_ref[1], place_ref[2]
    copies = []

    def add(source, device_y, device_z, start, count):
        e = lax.rem(device_y + 2 * NY, NY) * NZ + lax.rem(device_z + 2 * NZ, NZ)
        copies.append(
            pltpu.make_async_copy(
                source, gathered.at[e, pl.ds(start, count)], sems.at[len(copies) % 8]
            )
        )

    for i, dy in enumerate(Y_FROM):
        for j, dz in enumerate(Z_FROM):
            if i < 3:
                source = a_refs[i].at[pl.ds(j * PART_A, PART_A)]
            else:
                source = a_refs[3 + j // 4].at[pl.ds(j % 4 * PART_A, PART_A)]
            add(source, y + dy, z + dz, 0, PART_A)
    for j, dz in enumerate(Z_FROM):
        for i, dy in enumerate(Y_FROM):
            if j < 7:
                source = b_refs[j].at[pl.ds(i * PART_B, PART_B)]
            else:
                source = b_refs[7 + i // 2].at[pl.ds(i % 2 * PART_B, PART_B)]
            add(source, y + dy, z + dz, PART_A, PART_B)
    return copies


def expert_kernel(*refs):
    place_ref = refs[0]
    pieces = refs[1:15]
    rows_ref, tokens_ref, cot_ref, pick_ref, pair_ref = refs[15:20]
    big_ref, acts_ref = refs[20:22]
    gathered, weights, rows, picked, sems, row_sems = refs[22:]
    copies = block_copies(pieces, gathered, place_ref, sems)
    row_copies = [
        pltpu.make_async_copy(
            rows_ref.at[g], rows.at[:, pl.ds(g * COLS, COLS)], row_sems.at[g]
        )
        for g in range(N_DP)
    ]
    for copy in copies + row_copies:
        copy.start()
    unit = lax.broadcasted_iota(jnp.int32, (N_DP * PAD, UNITS), 1)
    pick = jnp.where(pick_ref[...] == unit, 1.0, 0.0).astype(BF16)
    for copy in copies:
        copy.wait()

    def assemble(g, carry):
        for half in range(2):
            j = 2 * g + half
            both = jnp.concatenate([gathered[2 * j], gathered[2 * j + 1]], axis=1)
            mixed = dot(both, pair_ref[...]).astype(BF16)
            lanes = pl.ds(pl.multiple_of(j * 128, 128), 128)
            for m in range(3):
                part = mixed[m * HALF : (m + 1) * HALF]
                weights[m, :HALF, lanes] = part[:, :128]
                weights[m, HALF:, lanes] = part[:, 128:]
        lanes = pl.ds(pl.multiple_of(g * COLS, COLS), COLS)
        for m in range(3):
            picked[m, :, lanes] = dot(pick, weights[m, :, lanes]).astype(BF16)
        return carry

    lax.fori_loop(0, N_DP, assemble, 0)

    shared_gate = dot_last(tokens_ref[...], weights[0])
    shared_up = dot_last(tokens_ref[...], weights[1])
    shared_dh = dot_last(cot_ref[...], weights[2])
    act, slope = silu_parts(shared_gate)
    shared_hidden = (act * shared_up).astype(BF16)
    shared_dgate = (shared_dh * shared_up * slope).astype(BF16)
    shared_dup = (shared_dh * act).astype(BF16)

    for copy in row_copies:
        copy.wait()
    gate = dot_last(picked[0], rows[:SLOTS])
    up = dot_last(picked[1], rows[:SLOTS])
    dh = dot_last(picked[2], rows[SLOTS:])
    act, slope = silu_parts(gate)
    hidden = act * up
    dgate = dh * up * slope
    dup = dh * act
    hidden_t = hidden.T.astype(BF16)
    dgate_t = dgate.T.astype(BF16)
    dup_t = dup.T.astype(BF16)
    for m, value in enumerate((dgate, dup, hidden)):
        value = value.astype(BF16)
        for s in range(N_DP):
            acts_ref[s, m * PAD : (m + 1) * PAD, :] = value[s * PAD : (s + 1) * PAD]

    def outputs(g, carry):
        lanes = pl.ds(pl.multiple_of(g * COLS, COLS), COLS)
        big_ref[g, :SLOTS, :] = dot(hidden_t, picked[2, :, lanes]).astype(BF16)
        big_ref[g, SLOTS:ROWS, :] = (
            dot(dgate_t, picked[0, :, lanes]) + dot(dup_t, picked[1, :, lanes])
        ).astype(BF16)
        big_ref[g, ROWS : ROWS + TOK, :] = dot(shared_hidden, weights[2, :, lanes]).astype(BF16)
        big_ref[g, ROWS + TOK :, :] = (
            dot(shared_dgate, weights[0, :, lanes]) + dot(shared_dup, weights[1, :, lanes])
        ).astype(BF16)
        return carry

    lax.fori_loop(0, N_DP, outputs, 0)


def grad_kernel(code_ref, acts_ref, rows_ref, out_ref):
    column = lax.broadcasted_iota(jnp.int32, (SHARE, N_DP * PAD), 1)
    order = jnp.where(code_ref[...] == column, 1.0, 0.0).astype(BF16)
    for m in range(3):
        acts = jnp.concatenate(
            [acts_ref[b, m * PAD : (m + 1) * PAD, :] for b in range(N_DP)], axis=0
        )
        mine = dot(order, acts).astype(BF16)
        start = SLOTS if m == 2 else 0
        for g in range(N_DP):
            out_ref[m, :, g * COLS : (g + 1) * COLS] = dot(
                mine, rows_ref[g, start : start + SLOTS, :]
            ).astype(BF16)


def gather_weights(dense_weights):
    packed = jnp.concatenate([dense_weights[:, :HALF], dense_weights[:, HALF:]], axis=2)
    packed = packed.reshape(3 * HALF, 128)

    def along_z(own):
        half = own.shape[0] // 2
        f1, b1 = shift(own, "z", 1), shift(own, "z", -1)
        f2, b2 = shift(own, "z", 2), shift(own, "z", -2)
        f3, b3 = shift(f2, "z", 1), shift(b2, "z", -1)
        return [own, f1, b1, f2, b2, f3, b3, shift(f2[:half], "z", 2), shift(b2[half:], "z", -2)]

    def along_y(own):
        half = own.shape[0] // 2
        f, b = shift(own, "y", 1), shift(own, "y", -1)
        return [own, f, b, shift(f[:half], "y", 1), shift(b[half:], "y", -1)]

    part_a = along_y(jnp.concatenate(along_z(packed[:PART_A])))
    part_b = along_z(jnp.concatenate(along_y(packed[PART_A:])))
    return part_a + part_b


def body(dense_weights, tokens, cotangent, routes, route_gates, unit_perm, slab_owner):
    g = lax.axis_index(DP)
    y, z = lax.axis_index("y"), lax.axis_index("z")
    place = jnp.stack([g, y, z]).astype(jnp.int32)
    pieces = gather_weights(dense_weights)

    owned = slab_owner[y * NZ + z]
    units = lax.dynamic_slice(unit_perm, (owned // 4, owned % 4 * EH), (1, EH)).reshape(N_DP, SHARE)
    block = units // UNITS
    inside = block == g
    rank = jnp.cumsum(inside.astype(jnp.int32), axis=1) - 1
    spot = jnp.arange(PAD, dtype=jnp.int32)
    taken = inside[:, None, :] & (rank[:, None, :] == spot[None, :, None])
    pick = jnp.sum(jnp.where(taken, (units - g * UNITS + 1)[:, None, :], 0), axis=2) - 1
    pick = pick.reshape(N_DP * PAD, 1)
    mine = lax.dynamic_index_in_dim(block, g, 0, keepdims=False)
    earlier = jnp.tril(jnp.ones((SHARE, SHARE), jnp.bool_), -1)
    code = mine * PAD + jnp.sum((mine[:, None] == mine[None, :]) & earlier, axis=1, dtype=jnp.int32)
    code = code.reshape(SHARE, 1)

    table, order = slot_columns(), order_matrix()
    send = pl.pallas_call(
        send_kernel,
        out_shape=jax.ShapeDtypeStruct((ROWS, COLS), BF16),
        in_specs=[smem()] + [vmem()] * 5,
        out_specs=vmem(),
        compiler_params=params(),
    )(place, routes, route_gates, table, tokens, cotangent)
    received = lax.all_to_all(
        send.reshape(N_EXP, 2 * CAP, COLS), EXPERT, split_axis=0, concat_axis=0, tiled=True
    ).reshape(ROWS, COLS)
    ordered = pl.pallas_call(
        order_in_kernel,
        out_shape=jax.ShapeDtypeStruct((ROWS, COLS), BF16),
        in_specs=[vmem()] * 2,
        out_specs=vmem(),
        compiler_params=params(),
    )(order, received)
    rows = lax.all_gather(ordered, DP, axis=0, tiled=False)

    big, acts = pl.pallas_call(
        expert_kernel,
        out_shape=(
            jax.ShapeDtypeStruct((N_DP, ROWS + 2 * TOK, COLS), BF16),
            jax.ShapeDtypeStruct((N_DP, 3 * PAD, SLOTS), BF16),
        ),
        in_specs=[smem()] + [hbm()] * 15 + [vmem()] * 4,
        out_specs=(vmem(), vmem()),
        scratch_shapes=[
            pltpu.VMEM((N_EXP, 3 * HALF, 128), BF16),
            pltpu.VMEM((3, UNITS, D), BF16),
            pltpu.VMEM((ROWS, D), BF16),
            pltpu.VMEM((3, N_DP * PAD, D), BF16),
            pltpu.SemaphoreType.DMA((8,)),
            pltpu.SemaphoreType.DMA((N_DP,)),
        ],
        compiler_params=params(),
    )(place, *pieces, rows, tokens, cotangent, pick, pair_matrix())

    sums = lax.psum_scatter(big, DP, scatter_dimension=0, tiled=False)
    sums = sums.reshape(ROWS + 2 * TOK, COLS)
    back = pl.pallas_call(
        order_out_kernel,
        out_shape=jax.ShapeDtypeStruct((ROWS, COLS), BF16),
        in_specs=[vmem()] * 2,
        out_specs=vmem(),
        compiler_params=params(),
    )(order, sums)
    back = lax.all_to_all(
        back.reshape(N_EXP, 2 * CAP, COLS), EXPERT, split_axis=0, concat_axis=0, tiled=True
    ).reshape(ROWS, COLS)
    mixed, token_grad = pl.pallas_call(
        combine_kernel,
        out_shape=(jax.ShapeDtypeStruct((TOK, COLS), BF16),) * 2,
        in_specs=[vmem()] * 5,
        out_specs=(vmem(), vmem()),
        compiler_params=params(),
    )(routes, route_gates, table, back, sums)

    acts = lax.all_to_all(acts, DP, split_axis=0, concat_axis=0, tiled=True)
    grads = pl.pallas_call(
        grad_kernel,
        out_shape=jax.ShapeDtypeStruct((3, SHARE, D), BF16),
        in_specs=[vmem()] * 3,
        out_specs=vmem(),
        compiler_params=params(),
    )(code, acts, rows)
    return mixed, token_grad, grads[None]


def solution(mesh):
    mesh = Mesh(mesh.devices.reshape(NX, NC, NY, NZ), ("x", "c", "y", "z"))
    in_specs = (
        P(None, DP, EXPERT),
        P(EXPERT, None),
        P(EXPERT, None),
        P(EXPERT, None),
        P(EXPERT, None),
        P(),
        P(),
    )
    out_specs = (P(EXPERT, DP), P(EXPERT, DP), P(EXPERT, None, DP, None))
    return jax.shard_map(body, mesh=mesh, in_specs=in_specs, out_specs=out_specs, check_vma=False)
```

```python
import jax
import jax.numpy as jnp
import numpy as np
from jax import lax
from jax.experimental import pallas as pl
from jax.experimental.pallas import tpu as pltpu
from jax.sharding import Mesh, PartitionSpec as P

NX, NC, NY, NZ = 4, 2, 4, 8
DP, EXPERT = ("x", "c"), ("y", "z")
SIZE = {"x": NX, "c": NC, "y": NY, "z": NZ}
D = 2048
EH = 1408
UNITS = 704
HALF = UNITS // 2
SHARE = 176
PICK = 22
PAD = 32
CAP = 20
TOK = 128
N_DP, N_EXP = 8, 32
SLOTS = N_EXP * CAP
ROWS = 2 * SLOTS
COLS = D // N_DP
SUM_ROWS = SLOTS + TOK
SUM_HALF = SUM_ROWS // 2
PART_A = 512
PART_B = 3 * HALF - PART_A
F32, BF16 = jnp.float32, jnp.bfloat16
VMEM_LIMIT = 60 * 1024 * 1024
Z_FROM = (0, -1, 1, -2, 2, -3, 3, 4)
Y_FROM = (0, -1, 1, 2)


def shift(value, axis, by):
    size = SIZE[axis]
    return lax.ppermute(value, axis, [(i, (i + by) % size) for i in range(size)])


def dot(lhs, rhs):
    return jnp.dot(lhs, rhs, preferred_element_type=F32)


def dot_last(lhs, rhs):
    return lax.dot_general(lhs, rhs, (((1,), (1,)), ((), ())), preferred_element_type=F32)


def dot_first(lhs, rhs):
    return lax.dot_general(lhs, rhs, (((0,), (0,)), ((), ())), preferred_element_type=F32)


def split3(value):
    high = value.astype(BF16)
    rest = value - high.astype(F32)
    middle = rest.astype(BF16)
    return high, middle, (rest - middle.astype(F32)).astype(BF16)


def silu_parts(preact):
    sigmoid_value = jax.nn.sigmoid(preact)
    return preact * sigmoid_value, sigmoid_value * (1.0 + preact * (1.0 - sigmoid_value))


def vmem():
    return pl.BlockSpec(memory_space=pltpu.VMEM)


def smem():
    return pl.BlockSpec(memory_space=pltpu.SMEM)


def hbm():
    return pl.BlockSpec(memory_space=pl.ANY)


def params():
    return pltpu.CompilerParams(vmem_limit_bytes=VMEM_LIMIT)


def slot_columns():
    column = np.arange(ROWS)
    table = np.zeros((8, ROWS), np.int32)
    table[0] = column // (2 * CAP)
    table[1] = column % (2 * CAP) // CAP
    table[2] = column % CAP
    return jnp.asarray(table)


def order_matrix():
    matrix = np.zeros((160, 160), np.float32)
    for b in range(4):
        for p in range(2):
            for r in range(CAP):
                matrix[p * 80 + b * CAP + r, b * 40 + p * CAP + r] = 1
    return jnp.asarray(matrix, BF16)


def pair_matrix():
    matrix = np.zeros((256, 256), np.float32)
    for i in range(64):
        matrix[i, i] = 1
        matrix[64 + i, 128 + i] = 1
        matrix[128 + i, 64 + i] = 1
        matrix[192 + i, 192 + i] = 1
    return jnp.asarray(matrix, BF16)


def slot_masks(routes_ref, gates_ref, table_ref):
    expert = table_ref[0:1, :]
    part = table_ref[1:2, :]
    rank = table_ref[2:3, :].astype(F32)
    named = jnp.zeros((TOK, ROWS), F32)
    gate = jnp.zeros((TOK, ROWS), F32)
    for k in range(4):
        hit = routes_ref[:, k : k + 1] == expert
        named = named + jnp.where(hit, 1.0, 0.0)
        gate = gate + jnp.where(hit, gates_ref[:, k : k + 1], 0.0)
    row = lax.broadcasted_iota(jnp.int32, (TOK, TOK), 0)
    col = lax.broadcasted_iota(jnp.int32, (TOK, TOK), 1)
    before = jnp.where(col < row, 1.0, 0.0).astype(BF16)
    place = dot(before, named.astype(BF16))
    slot = jnp.where((place == rank) & (named > 0.5), 1.0, 0.0)
    first = jnp.where(part == 0, slot, 0.0)
    second = jnp.where(part == 1, slot, 0.0)
    return first, second, gate


def send_kernel(place_ref, routes_ref, gates_ref, table_ref, tokens_ref, cot_ref, out_ref):
    first, second, gate = slot_masks(routes_ref, gates_ref, table_ref)
    columns = pl.ds(pl.multiple_of(place_ref[0] * COLS, COLS), COLS)
    rows_x = dot_first(first.astype(BF16), tokens_ref[:, columns])
    rows_dy = dot_first(second.astype(BF16), cot_ref[:, columns])
    ones = jnp.ones((TOK, COLS), BF16)
    scale = jnp.zeros((ROWS, COLS), F32)
    for piece in split3(second * gate):
        scale = scale + dot_first(piece, ones)
    out_ref[...] = (rows_x + rows_dy * scale).astype(BF16)


def order_in_kernel(order_ref, in_ref, out_ref):
    for b in range(8):
        rows = dot(order_ref[...], in_ref[160 * b : 160 * (b + 1), :]).astype(BF16)
        out_ref[80 * b : 80 * (b + 1), :] = rows[:80]
        out_ref[SLOTS + 80 * b : SLOTS + 80 * (b + 1), :] = rows[80:]


def sum_pair_kernel(keep_ref, got_ref, own_ref, next_ref, last_ref, far_up_ref, far_down_ref):
    def total(i, rows=slice(None)):
        return (keep_ref[i, rows].astype(F32) + got_ref[i, rows].astype(F32)).astype(BF16)

    own_ref[...] = total(0)
    next_ref[...] = total(1)
    last_ref[...] = total(3)
    far_up_ref[...] = total(2, slice(0, SUM_HALF))
    far_down_ref[...] = total(2, slice(SUM_HALF, SUM_ROWS))


def sum_far_kernel(next_ref, last_ref, up_ref, down_ref, next_out, last_out):
    top, bottom = slice(0, SUM_HALF), slice(SUM_HALF, SUM_ROWS)
    next_out[top] = (next_ref[top].astype(F32) + up_ref[...].astype(F32)).astype(BF16)
    next_out[bottom] = next_ref[bottom]
    last_out[top] = last_ref[top]
    last_out[bottom] = (last_ref[bottom].astype(F32) + down_ref[...].astype(F32)).astype(BF16)


def sum_last_kernel(*refs):
    order_ref, out_refs, back_refs = refs[0], refs[1:4], refs[4:7]
    rows_ref, own_ref = refs[7:]

    def total(parts, rows):
        return sum(part[rows].astype(F32) for part in parts)

    for b in range(8):
        rows = slice(80 * b, 80 * (b + 1))
        both = jnp.concatenate([total(out_refs, rows), total(back_refs, rows)], axis=0)
        rows_ref[160 * b : 160 * (b + 1), :] = dot_first(
            order_ref[...], both.astype(BF16)
        ).astype(BF16)
    rows = slice(SLOTS, SLOTS + TOK)
    own_ref[0] = total(out_refs, rows)
    own_ref[1] = total(back_refs, rows)


def combine_kernel(routes_ref, gates_ref, table_ref, back_ref, own_ref, mixed_ref, grad_ref):
    first, second, gate = slot_masks(routes_ref, gates_ref, table_ref)
    rows = back_ref[...]
    mixed = own_ref[0]
    for piece in split3(first * gate):
        mixed = mixed + dot(piece, rows)
    mixed_ref[...] = mixed.astype(BF16)
    grad_ref[...] = (own_ref[1] + dot(second.astype(BF16), rows)).astype(BF16)


def block_copies(refs, gathered, place_ref, sems):
    a_refs, b_refs = refs[:5], refs[5:]
    y, z = place_ref[1], place_ref[2]
    copies = []

    def add(source, device_y, device_z, start, count):
        e = lax.rem(device_y + 2 * NY, NY) * NZ + lax.rem(device_z + 2 * NZ, NZ)
        copies.append(
            pltpu.make_async_copy(
                source, gathered.at[e, pl.ds(start, count)], sems.at[0 if start == 0 else 1, e]
            )
        )

    for i, dy in enumerate(Y_FROM):
        for j in range(NZ):
            if i < 3:
                source = a_refs[i].at[pl.ds(j * PART_A, PART_A)]
            else:
                source = a_refs[3 + j // 4].at[pl.ds(j % 4 * PART_A, PART_A)]
            add(source, y + dy, j, 0, PART_A)
    for j, dz in enumerate(Z_FROM):
        for i, dy in enumerate(Y_FROM):
            if j < 7:
                source = b_refs[j].at[pl.ds(i * PART_B, PART_B)]
            else:
                source = b_refs[7 + i // 2].at[pl.ds(i % 2 * PART_B, PART_B)]
            add(source, y + dy, z + dz, PART_A, PART_B)
    return copies


def expert_kernel(*refs):
    place_ref = refs[0]
    pieces = refs[1:15]
    rows_ref, tokens_ref, cot_ref, pick_ref, pair_ref = refs[15:20]
    sum_refs, acts_ref = refs[20:24], refs[24]
    gathered, weights, rows, picked, sums, sems, row_sems, sum_sems = refs[25:]
    copies = block_copies(pieces, gathered, place_ref, sems)
    row_copies = [
        pltpu.make_async_copy(
            rows_ref.at[g], rows.at[:, pl.ds(g * COLS, COLS)], row_sems.at[g]
        )
        for g in range(N_DP)
    ]
    for copy in copies + row_copies:
        copy.start()
    unit = lax.broadcasted_iota(jnp.int32, (N_DP * PAD, UNITS), 1)
    pick = jnp.where(pick_ref[...] == unit, 1.0, 0.0).astype(BF16)

    def assemble(g, carry):
        for i in range(4):
            for k, (start, count) in enumerate(((0, PART_A), (PART_A, PART_B))):
                block = gathered.at[4 * g + i, pl.ds(start, count)]
                pltpu.make_async_copy(block, block, sems.at[k, 4 * g + i]).wait()
        for half in range(2):
            j = 2 * g + half
            low, high = gathered[2 * j], gathered[2 * j + 1]
            mixed = jnp.concatenate([low[:, :64], high[:, :64], low[:, 64:], high[:, 64:]], axis=1)
            lanes = pl.ds(pl.multiple_of(j * 128, 128), 128)
            for m in range(3):
                part = mixed[m * HALF : (m + 1) * HALF]
                weights[m, :HALF, lanes] = part[:, :128]
                weights[m, HALF:, lanes] = part[:, 128:]
        lanes = pl.ds(pl.multiple_of(g * COLS, COLS), COLS)
        for m in range(3):
            picked[m, :, lanes] = dot(pick, weights[m, :, lanes]).astype(BF16)
        return carry

    lax.fori_loop(0, N_DP, assemble, 0, unroll=2)

    shared_gate = dot_last(tokens_ref[...], weights[0])
    shared_up = dot_last(tokens_ref[...], weights[1])
    shared_dh = dot_last(cot_ref[...], weights[2])
    act, slope = silu_parts(shared_gate)
    shared_hidden = (act * shared_up).astype(BF16)
    shared_dgate = (shared_dh * shared_up * slope).astype(BF16)
    shared_dup = (shared_dh * act).astype(BF16)

    for copy in row_copies:
        copy.wait()
    gate = dot_last(picked[0], rows[:SLOTS])
    up = dot_last(picked[1], rows[:SLOTS])
    dh = dot_last(picked[2], rows[SLOTS:])
    act, slope = silu_parts(gate)
    hidden = act * up
    dgate = dh * up * slope
    dup = dh * act
    hidden_t = hidden.T.astype(BF16)
    dgate_t = dgate.T.astype(BF16)
    dup_t = dup.T.astype(BF16)
    for m, value in enumerate((dgate, dup, hidden)):
        value = value.astype(BF16)
        for s in range(N_DP):
            acts_ref[s, m * PAD : (m + 1) * PAD, :] = value[s * PAD : (s + 1) * PAD]

    x, c = place_ref[0] // NC, place_ref[0] % NC

    def sum_copy(part, k, i):
        return pltpu.make_async_copy(
            sums.at[part, k, i], sum_refs[2 * part + k].at[i], sum_sems.at[part, k, i]
        )

    def outputs(i, carry):
        for k in range(NC):
            g = lax.rem(x + i, NX) * NC + (c if k == 0 else 1 - c)
            lanes = pl.ds(pl.multiple_of(g * COLS, COLS), COLS)
            sums[0, k, i, :SLOTS, :] = dot(hidden_t, picked[2, :, lanes]).astype(BF16)
            sums[0, k, i, SLOTS:, :] = dot(shared_hidden, weights[2, :, lanes]).astype(BF16)
            sum_copy(0, k, i).start()
            sums[1, k, i, :SLOTS, :] = (
                dot(dgate_t, picked[0, :, lanes]) + dot(dup_t, picked[1, :, lanes])
            ).astype(BF16)
            sums[1, k, i, SLOTS:, :] = (
                dot(shared_dgate, weights[0, :, lanes]) + dot(shared_dup, weights[1, :, lanes])
            ).astype(BF16)
            sum_copy(1, k, i).start()
        return carry

    lax.fori_loop(0, NX, outputs, 0)
    for part in range(2):
        for k in range(NC):
            for i in range(NX):
                sum_copy(part, k, i).wait()


def grad_kernel(code_ref, acts_ref, rows_ref, out_ref):
    column = lax.broadcasted_iota(jnp.int32, (SHARE, N_DP * PAD), 1)
    order = jnp.where(code_ref[...] == column, 1.0, 0.0).astype(BF16)
    for m in range(3):
        acts = jnp.concatenate(
            [acts_ref[b, m * PAD : (m + 1) * PAD, :] for b in range(N_DP)], axis=0
        )
        mine = dot(order, acts).astype(BF16)
        start = SLOTS if m == 2 else 0
        for g in range(N_DP):
            out_ref[m, :, g * COLS : (g + 1) * COLS] = dot(
                mine, rows_ref[g, start : start + SLOTS, :]
            ).astype(BF16)


def stack_kernel(*refs):
    sources, target = refs[:5], refs[5]
    start = 0
    for source in sources:
        count = source.shape[0]
        target[start : start + count, :] = source[...]
        start += count


def tie(values, *others):
    return lax.optimization_barrier((tuple(values),) + others)


def pack_weights(dense_weights):
    packed = jnp.concatenate([dense_weights[:, :HALF], dense_weights[:, HALF:]], axis=2)
    return packed.reshape(3 * HALF, 128)


def ends_two(own, axis, by):
    f2, b2 = own
    half = f2.shape[0] // 2
    return shift(f2[:half], axis, by), shift(b2[half:], axis, -by)


def body(dense_weights, tokens, cotangent, routes, route_gates, unit_perm, slab_owner):
    g = lax.axis_index(DP)
    y, z = lax.axis_index("y"), lax.axis_index("z")
    place = jnp.stack([g, y, z]).astype(jnp.int32)
    packed = pack_weights(dense_weights)
    a0, b0 = packed[:PART_A], packed[PART_A:]
    part_a = lax.all_gather(a0, "z", axis=0, tiled=True)
    b_f, b_b = shift(b0, "y", 1), shift(b0, "y", -1)

    owned = slab_owner[y * NZ + z]
    units = lax.dynamic_slice(unit_perm, (owned // 4, owned % 4 * EH), (1, EH)).reshape(N_DP, SHARE)
    block = units // UNITS
    inside = block == g
    rank = jnp.cumsum(inside.astype(jnp.int32), axis=1) - 1
    spot = jnp.arange(PAD, dtype=jnp.int32)
    taken = inside[:, None, :] & (rank[:, None, :] == spot[None, :, None])
    pick = jnp.sum(jnp.where(taken, (units - g * UNITS + 1)[:, None, :], 0), axis=2) - 1
    pick = pick.reshape(N_DP * PAD, 1)
    mine = lax.dynamic_index_in_dim(block, g, 0, keepdims=False)
    earlier = jnp.tril(jnp.ones((SHARE, SHARE), jnp.bool_), -1)
    code = mine * PAD + jnp.sum((mine[:, None] == mine[None, :]) & earlier, axis=1, dtype=jnp.int32)
    code = code.reshape(SHARE, 1)

    table, order = slot_columns(), order_matrix()
    send = pl.pallas_call(
        send_kernel,
        out_shape=jax.ShapeDtypeStruct((ROWS, COLS), BF16),
        in_specs=[smem()] + [vmem()] * 5,
        out_specs=vmem(),
        compiler_params=params(),
    )(place, routes, route_gates, table, tokens, cotangent)
    received = lax.all_to_all(
        send.reshape(N_EXP, 2 * CAP, COLS), EXPERT, split_axis=0, concat_axis=0, tiled=True
    ).reshape(ROWS, COLS)
    part_b = pl.pallas_call(
        stack_kernel,
        out_shape=jax.ShapeDtypeStruct((NY * PART_B, 128), BF16),
        in_specs=[vmem()] * 5,
        out_specs=vmem(),
        compiler_params=params(),
    )(b0, b_f, b_b, *ends_two((b_f, b_b), "y", 1))
    part_a, _ = lax.optimization_barrier((part_a, received))
    received, _ = lax.optimization_barrier((received, part_b))
    a_f, a_b = shift(part_a, "y", 1), shift(part_a, "y", -1)
    b_f1, b_b1 = shift(part_b, "z", 1), shift(part_b, "z", -1)
    b_f2, b_b2 = shift(b_f1, "z", 1), shift(b_b1, "z", -1)
    b_f3, b_b3 = shift(b_f2, "z", 1), shift(b_b2, "z", -1)
    pieces_b = [part_b, b_f1, b_b1, b_f2, b_b2, b_f3, b_b3]
    a_f, a_b, b_f2, b_b2 = lax.optimization_barrier((a_f, a_b, b_f2, b_b2))
    pieces = [part_a, a_f, a_b, *ends_two((a_f, a_b), "y", 1)] + pieces_b
    pieces += ends_two((b_f3, b_b3), "z", 1)
    ordered = pl.pallas_call(
        order_in_kernel,
        out_shape=jax.ShapeDtypeStruct((ROWS, COLS), BF16),
        in_specs=[vmem()] * 2,
        out_specs=vmem(),
        compiler_params=params(),
    )(order, received)
    rows = lax.all_gather(ordered, DP, axis=0, tiled=False)

    keep_out, give_out, keep_back, give_back, acts = pl.pallas_call(
        expert_kernel,
        out_shape=(jax.ShapeDtypeStruct((NX, SUM_ROWS, COLS), BF16),) * 4
        + (
            jax.ShapeDtypeStruct((N_DP, 3 * PAD, SLOTS), BF16),
        ),
        in_specs=[smem()] + [hbm()] * 15 + [vmem()] * 4,
        out_specs=(hbm(),) * 4 + (vmem(),),
        scratch_shapes=[
            pltpu.VMEM((N_EXP, 3 * HALF, 128), BF16),
            pltpu.VMEM((3, UNITS, D), BF16),
            pltpu.VMEM((ROWS, D), BF16),
            pltpu.VMEM((3, N_DP * PAD, D), BF16),
            pltpu.VMEM((2, NC, NX, SUM_ROWS, COLS), BF16),
            pltpu.SemaphoreType.DMA((2, N_EXP)),
            pltpu.SemaphoreType.DMA((N_DP,)),
            pltpu.SemaphoreType.DMA((2, NC, NX)),
        ],
        compiler_params=params(),
    )(place, *pieces, rows, tokens, cotangent, pick, pair_matrix())

    def local(kernel, shapes, *values):
        return pl.pallas_call(
            kernel,
            out_shape=tuple(jax.ShapeDtypeStruct(*shape) for shape in shapes),
            in_specs=[vmem()] * len(values),
            out_specs=(vmem(),) * len(shapes),
            compiler_params=params(),
        )(*values)

    whole, half = ((SUM_ROWS, COLS), BF16), ((SUM_HALF, COLS), BF16)

    def near(keep, got):
        return local(sum_pair_kernel, [whole] * 3 + [half] * 2, keep, got)

    def far(parts):
        own, following, last, up, down = parts
        following, last = local(
            sum_far_kernel, [whole] * 2, following, last, shift(up, "x", 1), shift(down, "x", -1)
        )
        return own, shift(following, "x", 1), shift(last, "x", -1)

    out_parts = far(near(keep_out, shift(give_out, "c", 1)))
    back_parts = far(near(keep_back, shift(give_back, "c", 1)))
    back, own = local(
        sum_last_kernel,
        [((ROWS, COLS), BF16), ((2, TOK, COLS), F32)],
        order,
        *out_parts,
        *back_parts,
    )
    back = lax.all_to_all(
        back.reshape(N_EXP, 2 * CAP, COLS), EXPERT, split_axis=0, concat_axis=0, tiled=True
    ).reshape(ROWS, COLS)
    mixed, token_grad = pl.pallas_call(
        combine_kernel,
        out_shape=(jax.ShapeDtypeStruct((TOK, COLS), BF16),) * 2,
        in_specs=[vmem()] * 5,
        out_specs=(vmem(), vmem()),
        compiler_params=params(),
    )(routes, route_gates, table, back, own)

    acts = lax.all_to_all(acts, DP, split_axis=0, concat_axis=0, tiled=True)
    grads = pl.pallas_call(
        grad_kernel,
        out_shape=jax.ShapeDtypeStruct((3, SHARE, D), BF16),
        in_specs=[vmem()] * 3,
        out_specs=vmem(),
        compiler_params=params(),
    )(code, acts, rows)
    return mixed, token_grad, grads[None]


def solution(mesh):
    mesh = Mesh(mesh.devices.reshape(NX, NC, NY, NZ), ("x", "c", "y", "z"))
    in_specs = (
        P(None, DP, EXPERT),
        P(EXPERT, None),
        P(EXPERT, None),
        P(EXPERT, None),
        P(EXPERT, None),
        P(),
        P(),
    )
    out_specs = (P(EXPERT, DP), P(EXPERT, DP), P(EXPERT, None, DP, None))
    return jax.shard_map(body, mesh=mesh, in_specs=in_specs, out_specs=out_specs, check_vma=False)
```

```python
import jax
import jax.numpy as jnp
import numpy as np
from jax import lax
from jax.experimental import pallas as pl
from jax.experimental.pallas import tpu as pltpu
from jax.sharding import Mesh, PartitionSpec as P

NX, NC, NY, NZ = 4, 2, 4, 8
DP, EXPERT = ("x", "c"), ("y", "z")
SIZE = {"x": NX, "c": NC, "y": NY, "z": NZ}
D = 2048
EH = 1408
UNITS = 704
HALF = UNITS // 2
SHARE = 176
PICK = 22
PAD = 32
CAP = 20
TOK = 128
N_DP, N_EXP = 8, 32
SLOTS = N_EXP * CAP
ROWS = 2 * SLOTS
COLS = D // N_DP
SUM_ROWS = SLOTS + TOK
SUM_HALF = SUM_ROWS // 2
PART_A = 512
PART_B = 3 * HALF - PART_A
F32, BF16 = jnp.float32, jnp.bfloat16
VMEM_LIMIT = 60 * 1024 * 1024
Z_FROM = (0, -1, 1, -2, 2, -3, 3, 4)
Y_FROM = (0, -1, 1, 2)


def shift(value, axis, by):
    size = SIZE[axis]
    return lax.ppermute(value, axis, [(i, (i + by) % size) for i in range(size)])


def dot(lhs, rhs):
    return jnp.dot(lhs, rhs, preferred_element_type=F32)


def dot_last(lhs, rhs):
    return lax.dot_general(lhs, rhs, (((1,), (1,)), ((), ())), preferred_element_type=F32)


def dot_first(lhs, rhs):
    return lax.dot_general(lhs, rhs, (((0,), (0,)), ((), ())), preferred_element_type=F32)


def split3(value):
    high = value.astype(BF16)
    rest = value - high.astype(F32)
    middle = rest.astype(BF16)
    return high, middle, (rest - middle.astype(F32)).astype(BF16)


def silu_parts(preact):
    sigmoid_value = jax.nn.sigmoid(preact)
    return preact * sigmoid_value, sigmoid_value * (1.0 + preact * (1.0 - sigmoid_value))


def vmem():
    return pl.BlockSpec(memory_space=pltpu.VMEM)


def smem():
    return pl.BlockSpec(memory_space=pltpu.SMEM)


def hbm():
    return pl.BlockSpec(memory_space=pl.ANY)


def params():
    return pltpu.CompilerParams(vmem_limit_bytes=VMEM_LIMIT)


def slot_columns():
    column = np.arange(ROWS)
    table = np.zeros((8, ROWS), np.int32)
    table[0] = column // (2 * CAP)
    table[1] = column % (2 * CAP) // CAP
    table[2] = column % CAP
    return jnp.asarray(table)


def order_matrix():
    matrix = np.zeros((160, 160), np.float32)
    for b in range(4):
        for p in range(2):
            for r in range(CAP):
                matrix[p * 80 + b * CAP + r, b * 40 + p * CAP + r] = 1
    return jnp.asarray(matrix, BF16)


def pair_matrix():
    matrix = np.zeros((256, 256), np.float32)
    for i in range(64):
        matrix[i, i] = 1
        matrix[64 + i, 128 + i] = 1
        matrix[128 + i, 64 + i] = 1
        matrix[192 + i, 192 + i] = 1
    return jnp.asarray(matrix, BF16)


def slot_masks(routes_ref, gates_ref, table_ref):
    expert = table_ref[0:1, :]
    part = table_ref[1:2, :]
    rank = table_ref[2:3, :].astype(F32)
    named = jnp.zeros((TOK, ROWS), F32)
    gate = jnp.zeros((TOK, ROWS), F32)
    for k in range(4):
        hit = routes_ref[:, k : k + 1] == expert
        named = named + jnp.where(hit, 1.0, 0.0)
        gate = gate + jnp.where(hit, gates_ref[:, k : k + 1], 0.0)
    row = lax.broadcasted_iota(jnp.int32, (TOK, TOK), 0)
    col = lax.broadcasted_iota(jnp.int32, (TOK, TOK), 1)
    before = jnp.where(col < row, 1.0, 0.0).astype(BF16)
    place = dot(before, named.astype(BF16))
    slot = jnp.where((place == rank) & (named > 0.5), 1.0, 0.0)
    first = jnp.where(part == 0, slot, 0.0)
    second = jnp.where(part == 1, slot, 0.0)
    return first, second, gate


def send_kernel(place_ref, routes_ref, gates_ref, table_ref, tokens_ref, cot_ref, out_ref):
    first, second, gate = slot_masks(routes_ref, gates_ref, table_ref)
    columns = pl.ds(pl.multiple_of(place_ref[0] * COLS, COLS), COLS)
    rows_x = dot_first(first.astype(BF16), tokens_ref[:, columns])
    rows_dy = dot_first(second.astype(BF16), cot_ref[:, columns])
    ones = jnp.ones((TOK, COLS), BF16)
    scale = jnp.zeros((ROWS, COLS), F32)
    for piece in split3(second * gate):
        scale = scale + dot_first(piece, ones)
    out_ref[...] = (rows_x + rows_dy * scale).astype(BF16)


def order_in_kernel(order_ref, in_ref, out_ref):
    for b in range(8):
        rows = dot(order_ref[...], in_ref[160 * b : 160 * (b + 1), :]).astype(BF16)
        out_ref[80 * b : 80 * (b + 1), :] = rows[:80]
        out_ref[SLOTS + 80 * b : SLOTS + 80 * (b + 1), :] = rows[80:]


def sum_pair_kernel(
    keep_ref, got_ref, own_ref, next_ref, last_ref, up_ref, down_ref, kept, got, sems, out_sems
):
    steps = (2, 1, 3, 0)

    def loads(i):
        return (
            pltpu.make_async_copy(keep_ref.at[i], kept.at[i], sems.at[0, i]),
            pltpu.make_async_copy(got_ref.at[i], got.at[i], sems.at[1, i]),
        )

    def stores(i):
        if i == 2:
            return (
                pltpu.make_async_copy(kept.at[2, pl.ds(0, SUM_HALF)], up_ref, out_sems.at[2]),
                pltpu.make_async_copy(
                    kept.at[2, pl.ds(SUM_HALF, SUM_HALF)], down_ref, out_sems.at[4]
                ),
            )
        target = {0: own_ref, 1: next_ref, 3: last_ref}[i]
        return (pltpu.make_async_copy(kept.at[i], target, out_sems.at[i]),)

    for i in steps:
        for copy in loads(i):
            copy.start()
    for i in steps:
        for copy in loads(i):
            copy.wait()
        kept[i] = (kept[i].astype(F32) + got[i].astype(F32)).astype(BF16)
        for copy in stores(i):
            copy.start()
    for i in steps:
        for copy in stores(i):
            copy.wait()


def sum_far_kernel(next_ref, last_ref, up_ref, down_ref, next_out, last_out, ours, theirs, sems):
    places = ((next_ref, up_ref, next_out, 0), (last_ref, down_ref, last_out, SUM_HALF))
    loads, stores = [], []
    for k, (near_ref, far_ref, out_ref, start) in enumerate(places):
        rows = pl.ds(start, SUM_HALF)
        loads.append(pltpu.make_async_copy(near_ref.at[rows], ours.at[k], sems.at[0, k]))
        loads.append(pltpu.make_async_copy(far_ref, theirs.at[k], sems.at[1, k]))
        stores.append(pltpu.make_async_copy(ours.at[k], out_ref.at[rows], sems.at[2, k]))
    for copy in loads:
        copy.start()
    for k in range(2):
        loads[2 * k].wait()
        loads[2 * k + 1].wait()
        ours[k] = (ours[k].astype(F32) + theirs[k].astype(F32)).astype(BF16)
        stores[k].start()
    for copy in stores:
        copy.wait()


def sum_last_kernel(*refs):
    order_ref, out_refs, back_refs = refs[0], refs[1:4], refs[4:7]
    rows_ref, own_ref = refs[7:]

    def total(parts, rows):
        return sum(part[rows].astype(F32) for part in parts)

    for b in range(8):
        rows = slice(80 * b, 80 * (b + 1))
        both = jnp.concatenate([total(out_refs, rows), total(back_refs, rows)], axis=0)
        rows_ref[160 * b : 160 * (b + 1), :] = dot_first(
            order_ref[...], both.astype(BF16)
        ).astype(BF16)
    rows = slice(SLOTS, SLOTS + TOK)
    own_ref[0] = total(out_refs, rows)
    own_ref[1] = total(back_refs, rows)


def combine_kernel(routes_ref, gates_ref, table_ref, back_ref, own_ref, mixed_ref, grad_ref):
    first, second, gate = slot_masks(routes_ref, gates_ref, table_ref)
    rows = back_ref[...]
    mixed = own_ref[0]
    for piece in split3(first * gate):
        mixed = mixed + dot(piece, rows)
    mixed_ref[...] = mixed.astype(BF16)
    grad_ref[...] = (own_ref[1] + dot(second.astype(BF16), rows)).astype(BF16)


def block_copies(refs, gathered, place_ref, sems):
    a_refs, b_refs = refs[:5], refs[5:]
    y, z = place_ref[1], place_ref[2]
    copies = []

    def add(source, device_y, device_z, start, count):
        e = lax.rem(device_y + 2 * NY, NY) * NZ + lax.rem(device_z + 2 * NZ, NZ)
        copies.append(
            pltpu.make_async_copy(
                source, gathered.at[e, pl.ds(start, count)], sems.at[0 if start == 0 else 1, e]
            )
        )

    for i, dy in enumerate(Y_FROM):
        for j in range(NZ):
            if i < 3:
                source = a_refs[i].at[pl.ds(j * PART_A, PART_A)]
            else:
                source = a_refs[3 + j // 4].at[pl.ds(j % 4 * PART_A, PART_A)]
            add(source, y + dy, j, 0, PART_A)
    for j, dz in enumerate(Z_FROM):
        for i, dy in enumerate(Y_FROM):
            if j < 7:
                source = b_refs[j].at[pl.ds(i * PART_B, PART_B)]
            else:
                source = b_refs[7 + i // 2].at[pl.ds(i % 2 * PART_B, PART_B)]
            add(source, y + dy, z + dz, PART_A, PART_B)
    return copies


def expert_kernel(*refs):
    place_ref = refs[0]
    pieces = refs[1:15]
    rows_ref, tokens_ref, cot_ref, pick_ref, pair_ref = refs[15:20]
    sum_refs, acts_ref = refs[20:24], refs[24]
    gathered, weights, rows, picked, sums, sems, row_sems, sum_sems = refs[25:]
    copies = block_copies(pieces, gathered, place_ref, sems)
    row_copies = [
        pltpu.make_async_copy(
            rows_ref.at[g], rows.at[:, pl.ds(g * COLS, COLS)], row_sems.at[g]
        )
        for g in range(N_DP)
    ]
    for copy in copies + row_copies:
        copy.start()
    unit = lax.broadcasted_iota(jnp.int32, (N_DP * PAD, UNITS), 1)
    pick = jnp.where(pick_ref[...] == unit, 1.0, 0.0).astype(BF16)

    def assemble(g, carry):
        for i in range(4):
            for k, (start, count) in enumerate(((0, PART_A), (PART_A, PART_B))):
                block = gathered.at[4 * g + i, pl.ds(start, count)]
                pltpu.make_async_copy(block, block, sems.at[k, 4 * g + i]).wait()
        for half in range(2):
            j = 2 * g + half
            low, high = gathered[2 * j], gathered[2 * j + 1]
            mixed = jnp.concatenate([low[:, :64], high[:, :64], low[:, 64:], high[:, 64:]], axis=1)
            lanes = pl.ds(pl.multiple_of(j * 128, 128), 128)
            for m in range(3):
                part = mixed[m * HALF : (m + 1) * HALF]
                weights[m, :HALF, lanes] = part[:, :128]
                weights[m, HALF:, lanes] = part[:, 128:]
        lanes = pl.ds(pl.multiple_of(g * COLS, COLS), COLS)
        for m in range(3):
            picked[m, :, lanes] = dot(pick, weights[m, :, lanes]).astype(BF16)
        return carry

    lax.fori_loop(0, N_DP, assemble, 0, unroll=2)

    shared_gate = dot_last(tokens_ref[...], weights[0])
    shared_up = dot_last(tokens_ref[...], weights[1])
    shared_dh = dot_last(cot_ref[...], weights[2])
    act, slope = silu_parts(shared_gate)
    shared_hidden = (act * shared_up).astype(BF16)
    shared_dgate = (shared_dh * shared_up * slope).astype(BF16)
    shared_dup = (shared_dh * act).astype(BF16)

    for copy in row_copies:
        copy.wait()
    gate = dot_last(picked[0], rows[:SLOTS])
    up = dot_last(picked[1], rows[:SLOTS])
    dh = dot_last(picked[2], rows[SLOTS:])
    act, slope = silu_parts(gate)
    hidden = act * up
    dgate = dh * up * slope
    dup = dh * act
    x, c = place_ref[0] // NC, place_ref[0] % NC
    hidden_t = hidden.T.astype(BF16)
    dgate_t = dgate.T.astype(BF16)
    dup_t = dup.T.astype(BF16)
    for m, value in enumerate((dgate, dup, hidden)):
        value = value.astype(BF16)
        for s in range(N_DP):
            step = lax.rem(s // NC - x + NX, NX)
            other = lax.rem(s % NC + c, NC)
            acts_ref[other, step, m * PAD : (m + 1) * PAD, :] = value[s * PAD : (s + 1) * PAD]

    def sum_copy(part, k, i):
        return pltpu.make_async_copy(
            sums.at[part, k, i], sum_refs[2 * part + k].at[i], sum_sems.at[part, k, i]
        )

    def outputs(i, carry):
        for k in range(NC):
            g = lax.rem(x + i, NX) * NC + (c if k == 0 else 1 - c)
            lanes = pl.ds(pl.multiple_of(g * COLS, COLS), COLS)
            sums[0, k, i, :SLOTS, :] = dot(hidden_t, picked[2, :, lanes]).astype(BF16)
            sums[0, k, i, SLOTS:, :] = dot(shared_hidden, weights[2, :, lanes]).astype(BF16)
            sum_copy(0, k, i).start()
            sums[1, k, i, :SLOTS, :] = (
                dot(dgate_t, picked[0, :, lanes]) + dot(dup_t, picked[1, :, lanes])
            ).astype(BF16)
            sums[1, k, i, SLOTS:, :] = (
                dot(shared_dgate, weights[0, :, lanes]) + dot(shared_dup, weights[1, :, lanes])
            ).astype(BF16)
            sum_copy(1, k, i).start()
        return carry

    lax.fori_loop(0, NX, outputs, 0)
    for part in range(2):
        for k in range(NC):
            for i in range(NX):
                sum_copy(part, k, i).wait()


def merge_kernel(acts_ref, got_ref, *out_refs):
    for i in range(NX):
        out_refs[i][0] = acts_ref[0, i]
        out_refs[i][1] = got_ref[i]


def grad_kernel(code_ref, acts_0, acts_1, acts_2, acts_3, rows_ref, out_ref):
    acts_refs = (acts_0, acts_1, acts_2, acts_3)
    column = lax.broadcasted_iota(jnp.int32, (SHARE, N_DP * PAD), 1)
    order = jnp.where(code_ref[...] == column, 1.0, 0.0).astype(BF16)
    for m in range(3):
        acts = jnp.concatenate(
            [ref[k, m * PAD : (m + 1) * PAD, :] for ref in acts_refs for k in range(NC)], axis=0
        )
        mine = dot(order, acts).astype(BF16)
        start = SLOTS if m == 2 else 0
        for g in range(N_DP):
            out_ref[m, :, g * COLS : (g + 1) * COLS] = dot(
                mine, rows_ref[g, start : start + SLOTS, :]
            ).astype(BF16)


def stack_kernel(*refs):
    sources, target = refs[:5], refs[5]
    start = 0
    for source in sources:
        count = source.shape[0]
        target[start : start + count, :] = source[...]
        start += count


def tie(values, *others):
    return lax.optimization_barrier((tuple(values),) + others)


def pack_weights(dense_weights):
    packed = jnp.concatenate([dense_weights[:, :HALF], dense_weights[:, HALF:]], axis=2)
    return packed.reshape(3 * HALF, 128)


def ends_two(own, axis, by):
    f2, b2 = own
    half = f2.shape[0] // 2
    return shift(f2[:half], axis, by), shift(b2[half:], axis, -by)


def body(dense_weights, tokens, cotangent, routes, route_gates, unit_perm, slab_owner):
    g = lax.axis_index(DP)
    y, z = lax.axis_index("y"), lax.axis_index("z")
    place = jnp.stack([g, y, z]).astype(jnp.int32)
    packed = pack_weights(dense_weights)
    a0, b0 = packed[:PART_A], packed[PART_A:]
    part_a = lax.all_gather(a0, "z", axis=0, tiled=True)
    b_f, b_b = shift(b0, "y", 1), shift(b0, "y", -1)

    owned = slab_owner[y * NZ + z]
    units = lax.dynamic_slice(unit_perm, (owned // 4, owned % 4 * EH), (1, EH)).reshape(N_DP, SHARE)
    block = units // UNITS
    inside = block == g
    rank = jnp.cumsum(inside.astype(jnp.int32), axis=1) - 1
    spot = jnp.arange(PAD, dtype=jnp.int32)
    taken = inside[:, None, :] & (rank[:, None, :] == spot[None, :, None])
    pick = jnp.sum(jnp.where(taken, (units - g * UNITS + 1)[:, None, :], 0), axis=2) - 1
    pick = pick.reshape(N_DP * PAD, 1)
    mine = lax.dynamic_index_in_dim(block, g, 0, keepdims=False)
    earlier = jnp.tril(jnp.ones((SHARE, SHARE), jnp.bool_), -1)
    from_chip = (g // NC - mine // NC) % NX
    place_of = from_chip * NC + (mine % NC + g % NC) % NC
    code = place_of * PAD + jnp.sum((mine[:, None] == mine[None, :]) & earlier, axis=1, dtype=jnp.int32)
    code = code.reshape(SHARE, 1)

    table, order = slot_columns(), order_matrix()
    send = pl.pallas_call(
        send_kernel,
        out_shape=jax.ShapeDtypeStruct((ROWS, COLS), BF16),
        in_specs=[smem()] + [vmem()] * 5,
        out_specs=vmem(),
        compiler_params=params(),
    )(place, routes, route_gates, table, tokens, cotangent)
    received = lax.all_to_all(
        send.reshape(N_EXP, 2 * CAP, COLS), EXPERT, split_axis=0, concat_axis=0, tiled=True
    ).reshape(ROWS, COLS)
    part_b = pl.pallas_call(
        stack_kernel,
        out_shape=jax.ShapeDtypeStruct((NY * PART_B, 128), BF16),
        in_specs=[vmem()] * 5,
        out_specs=vmem(),
        compiler_params=params(),
    )(b0, b_f, b_b, *ends_two((b_f, b_b), "y", 1))
    part_a, _ = lax.optimization_barrier((part_a, received))
    received, _ = lax.optimization_barrier((received, part_b))
    a_f, a_b = shift(part_a, "y", 1), shift(part_a, "y", -1)
    b_f1, b_b1 = shift(part_b, "z", 1), shift(part_b, "z", -1)
    b_f2, b_b2 = shift(b_f1, "z", 1), shift(b_b1, "z", -1)
    b_f3, b_b3 = shift(b_f2, "z", 1), shift(b_b2, "z", -1)
    pieces_b = [part_b, b_f1, b_b1, b_f2, b_b2, b_f3, b_b3]
    a_f, a_b, b_f2, b_b2 = lax.optimization_barrier((a_f, a_b, b_f2, b_b2))
    pieces = [part_a, a_f, a_b, *ends_two((a_f, a_b), "y", 1)] + pieces_b
    pieces += ends_two((b_f3, b_b3), "z", 1)
    ordered = pl.pallas_call(
        order_in_kernel,
        out_shape=jax.ShapeDtypeStruct((ROWS, COLS), BF16),
        in_specs=[vmem()] * 2,
        out_specs=vmem(),
        compiler_params=params(),
    )(order, received)
    rows = lax.all_gather(ordered, DP, axis=0, tiled=False)

    keep_out, give_out, keep_back, give_back, acts = pl.pallas_call(
        expert_kernel,
        out_shape=(jax.ShapeDtypeStruct((NX, SUM_ROWS, COLS), BF16),) * 4
        + (
            jax.ShapeDtypeStruct((NC, NX, 3 * PAD, SLOTS), BF16),
        ),
        in_specs=[smem()] + [hbm()] * 15 + [vmem()] * 4,
        out_specs=(hbm(),) * 4 + (vmem(),),
        scratch_shapes=[
            pltpu.VMEM((N_EXP, 3 * HALF, 128), BF16),
            pltpu.VMEM((3, UNITS, D), BF16),
            pltpu.VMEM((ROWS, D), BF16),
            pltpu.VMEM((3, N_DP * PAD, D), BF16),
            pltpu.VMEM((2, NC, NX, SUM_ROWS, COLS), BF16),
            pltpu.SemaphoreType.DMA((2, N_EXP)),
            pltpu.SemaphoreType.DMA((N_DP,)),
            pltpu.SemaphoreType.DMA((2, NC, NX)),
        ],
        compiler_params=params(),
    )(place, *pieces, rows, tokens, cotangent, pick, pair_matrix())

    def local(kernel, shapes, *values):
        return pl.pallas_call(
            kernel,
            out_shape=tuple(jax.ShapeDtypeStruct(*shape) for shape in shapes),
            in_specs=[vmem()] * len(values),
            out_specs=(vmem(),) * len(shapes),
            compiler_params=params(),
        )(*values)

    whole, half = ((SUM_ROWS, COLS), BF16), ((SUM_HALF, COLS), BF16)

    def copied(kernel, shapes, scratch, aliases, *values):
        return pl.pallas_call(
            kernel,
            out_shape=tuple(jax.ShapeDtypeStruct(*shape) for shape in shapes),
            in_specs=[hbm()] * len(values),
            out_specs=(hbm(),) * len(shapes),
            scratch_shapes=scratch,
            input_output_aliases=aliases,
            compiler_params=params(),
        )(*values)

    def near(keep, got):
        scratch = [pltpu.VMEM((NX, SUM_ROWS, COLS), BF16)] * 2
        scratch += [pltpu.SemaphoreType.DMA((2, NX)), pltpu.SemaphoreType.DMA((NX + 1,))]
        return copied(sum_pair_kernel, [whole] * 3 + [half] * 2, scratch, {}, keep, got)

    def far(parts):
        own, following, last, up, down = parts
        scratch = [pltpu.VMEM((2, SUM_HALF, COLS), BF16)] * 2 + [pltpu.SemaphoreType.DMA((3, 2))]
        following, last = copied(
            sum_far_kernel,
            [whole] * 2,
            scratch,
            {0: 0, 1: 1},
            following,
            last,
            shift(up, "x", 1),
            shift(down, "x", -1),
        )
        return own, shift(following, "x", 1), shift(last, "x", -1)

    out_parts = far(near(keep_out, shift(give_out, "c", 1)))
    back_parts = far(near(keep_back, shift(give_back, "c", 1)))
    parts = local(
        merge_kernel, [((NC, 3 * PAD, SLOTS), BF16)] * NX, acts, shift(acts[1], "c", 1)
    )
    parts, own_back = tie(parts, back_parts[0])
    back_parts = (own_back,) + back_parts[1:]
    back, own = local(
        sum_last_kernel,
        [((ROWS, COLS), BF16), ((2, TOK, COLS), F32)],
        order,
        *out_parts,
        *back_parts,
    )
    back_sent = back
    back = lax.all_to_all(
        back.reshape(N_EXP, 2 * CAP, COLS), EXPERT, split_axis=0, concat_axis=0, tiled=True
    ).reshape(ROWS, COLS)
    mixed, token_grad = pl.pallas_call(
        combine_kernel,
        out_shape=(jax.ShapeDtypeStruct((TOK, COLS), BF16),) * 2,
        in_specs=[vmem()] * 5,
        out_specs=(vmem(), vmem()),
        compiler_params=params(),
    )(routes, route_gates, table, back, own)

    parts, _ = tie(parts, back_sent)
    acts = [parts[0], shift(parts[1], "x", 1), shift(parts[2], "x", 2), shift(parts[3], "x", -1)]
    grads = pl.pallas_call(
        grad_kernel,
        out_shape=jax.ShapeDtypeStruct((3, SHARE, D), BF16),
        in_specs=[vmem()] * 6,
        out_specs=vmem(),
        compiler_params=params(),
    )(code, *acts, rows)
    return mixed, token_grad, grads[None]


def solution(mesh):
    mesh = Mesh(mesh.devices.reshape(NX, NC, NY, NZ), ("x", "c", "y", "z"))
    in_specs = (
        P(None, DP, EXPERT),
        P(EXPERT, None),
        P(EXPERT, None),
        P(EXPERT, None),
        P(EXPERT, None),
        P(),
        P(),
    )
    out_specs = (P(EXPERT, DP), P(EXPERT, DP), P(EXPERT, None, DP, None))
    return jax.shard_map(body, mesh=mesh, in_specs=in_specs, out_specs=out_specs, check_vma=False)
```
